32 devices in a mesh: dp: 4 (over y, core), head: 8 (over z, x).
Axes of the slice: x: 2, y: 2, z: 4, core: 2. Of those that a mesh axis runs over, the one named last changes fastest.
Arguments:
- latent: bfloat16 [4096, 1536], P('dp', 'head'), may hold values from -6 to 6
- weight: bfloat16 [1536, 24576], P(None, 'head'), may hold values from -0.15625 to 0.15625
- query_grad: bfloat16 [4096, 24576], P('dp', 'head'), may hold values from -6 to 6
- master: float32 [1536, 24576], P('dp', 'head'), may hold values from -6 to 6
- first_moment: float32 [1536, 24576], P('dp', 'head'), may hold values from -6 to 6
- second_moment: float32 [1536, 24576], P('dp', 'head'), may hold values from 100 to 10000
Outputs:
- queries: bfloat16 [4096, 24576], P('dp', 'head')
- latent_grad: bfloat16 [4096, 1536], P('dp', 'head')
- new_master: float32 [1536, 24576], P('dp', 'head')
- new_first: float32 [1536, 24576], P('dp', 'head')
- new_second: float32 [1536, 24576], P('dp', 'head')
The draws below stay inside these ranges and needn't reach their ends.
All inputs are finite; a program needn't handle non-finite values.
Results may differ from the reference program's by a relative error of at most 0.014.
Values may be sent and summed in bfloat16 or wider, within the bound.
A program may use at most 128 MiB of HBM per device.

```python
import math
import jax
import jax.numpy as jnp
from jax import lax

D = 1536
TOK_DEV = 1024
STEP = 10
QW = 24576
TOKENS = 4096
N_HEAD = 8


def raised(result, rng, source, target, shards_of, factor):
    def block_of(position):
        return (jnp.arange(result.shape[position]) // (result.shape[position] // shards_of)).reshape((-1,) + (1,) * (result.ndim - 1 - position))

    first = jax.random.permutation(rng, shards_of)[block_of(target)]
    other_side = (block_of(target) + shards_of // 2) % shards_of
    return jnp.where((block_of(source) == first) | (block_of(source) == other_side), factor * result, result)


def shard_levels(key, shape, split, least, largest):
    def one(dim, blocks):
        steps = jax.random.uniform(jax.random.fold_in(jax.random.fold_in(key, 6), dim), (blocks,), jnp.float32, least / len(split), largest / len(split))
        return jnp.repeat(jnp.exp(steps), shape[dim] // blocks).reshape((-1,) + (1,) * (len(shape) - dim - 1))

    level = one(*split[0])
    for cut in split[1:]:
        level = level * one(*cut)
    return level


def scatter_about(own_key, shape, spread, most, shards=(), kind=jnp.bfloat16):
    array = spread * jax.random.normal(own_key, shape, jnp.float32)
    if shards:
        array = array * shard_levels(own_key, shape, shards, -0.22, 0.18)
    return jnp.clip(array, -most, most).astype(kind)


def bell_draw_with(key, extent, scale, limit, pieces, heavy, kind=jnp.bfloat16):
    drawn = scale * jax.random.normal(key, extent, jnp.float32)
    if pieces:
        drawn = drawn * shard_levels(key, extent, pieces, -0.22, 0.18)
    return jnp.clip(raised(drawn, jax.random.fold_in(key, 3), *heavy), -limit, limit).astype(kind)


def setup_inputs(seed: int = 0) -> dict:
    seeds = jax.random.split(jax.random.key(seed), 7)
    latent = bell_draw_with(seeds[0], (TOKENS, D), 1.0, 6.0, ((0, 4), (1, 8)), (0, 1, 8, 2.0))
    weight = scatter_about(seeds[1], (D, QW), D ** -0.5, 0.15625, ((1, 8),))
    query_grad = scatter_about(seeds[2], (TOKENS, QW), 1.0, 6.0, ((0, 4), (1, 8)))
    master = scatter_about(seeds[3], (D, QW), 1.0, 6.0, ((0, 4), (1, 8)), jnp.float32)
    first_moment = scatter_about(seeds[4], (D, QW), 1.0, 6.0, ((0, 4), (1, 8)), jnp.float32)
    second_moment = jnp.clip(jnp.exp(math.log(10000.0) - 4.6051702 * jax.random.uniform(seeds[5], (D, QW), jnp.float32) ** shard_levels(seeds[5], (D, QW), ((0, 4), (1, 8)), -0.2, 0.2)), 100.0, 10000.0)
    return dict(latent=latent, weight=weight, query_grad=query_grad, master=master, first_moment=first_moment, second_moment=second_moment)


def reference(latent, weight, query_grad, master, first_moment, second_moment):
    queries = jnp.dot(latent, weight, preferred_element_type=jnp.float32).astype(jnp.bfloat16)
    width = QW // N_HEAD

    def add_heads(total, index):
        start = (index * width).astype(jnp.int32)
        grad_cols = lax.dynamic_slice_in_dim(query_grad, start, width, 1)
        weight_cols = lax.dynamic_slice_in_dim(weight, start, width, 1)
        part = lax.dot_general(grad_cols, weight_cols, (((1,), (1,)), ((), ())), preferred_element_type=jnp.float32)
        return (total + part.astype(jnp.bfloat16).astype(jnp.float32), None)
    lat_total, unused = lax.scan(add_heads, jnp.zeros((TOKENS, D), jnp.float32), jnp.arange(N_HEAD, dtype=jnp.int32))
    latent_grad = lat_total.astype(jnp.bfloat16)
    groups = TOKENS // TOK_DEV
    lat_groups = latent.reshape(groups, TOK_DEV, D)
    grad_groups = query_grad.reshape(groups, TOK_DEV, QW)

    def add_group(total, index):
        lat_one = lax.dynamic_index_in_dim(lat_groups, index, 0, keepdims=False)
        grad_one = lax.dynamic_index_in_dim(grad_groups, index, 0, keepdims=False)
        part = lax.dot_general(lat_one, grad_one, (((0,), (0,)), ((), ())), preferred_element_type=jnp.float32)
        return (total + part.astype(jnp.bfloat16).astype(jnp.float32), None)
    grad, unused = lax.scan(add_group, jnp.zeros((D, QW), jnp.float32), jnp.arange(groups, dtype=jnp.int32))
    new_first = 0.9 * first_moment + 0.1 * grad
    new_second = 0.95 * second_moment + 0.05 * grad * grad
    first_hat = new_first / (1.0 - 0.9 ** STEP)
    second_hat = new_second / (1.0 - 0.95 ** STEP)
    new_master = master - 0.01 * (first_hat / (jnp.sqrt(second_hat) + 1e-08) + 0.1 * master)
    return (queries, latent_grad, new_master, new_first, new_second)
```

```python
import functools
import math

import jax
import jax.numpy as jnp
from jax import lax
from jax.experimental import pallas as pl
from jax.experimental.pallas import tpu as pltpu
from jax.sharding import PartitionSpec as P

STEP = 10
CORES = 2
MESH = pl.DeviceIdType.MESH


def flip(a, k):
    out = a
    b = 1
    while b <= k:
        if k & b:
            out = out + b * (1 - 2 * lax.rem(lax.div(a, b), 2))
        b *= 2
    return out


def kernel(sizes, lat_ref, w_hbm, qg_hbm, q_hbm, lg_ref, grad_ref,
           w, qg, lat, part, sib, ybuf, plat, xbuf, zbuf, lhs, qs,
           w_sem, qg_sem, own_sem, q_sem,
           az_s, az_r, ax_s, ax_r, lx_s, lx_r, lz_s, lz_r, ws_s, ws_r, wy_s, wy_r):
    Z, X, Y, R, NC, C, NT, T, NQ, TQ = sizes
    dp = lax.axis_index("dp")
    head = lax.axis_index("head")
    y, core = lax.div(dp, CORES), lax.rem(dp, CORES)
    z, x = lax.div(head, X), lax.rem(head, X)
    D = w_hbm.shape[0]
    rows = part.shape[2]
    B = lat.shape[2]
    f32 = jnp.float32

    def load_qg():
        return pltpu.make_async_copy(qg_hbm, qg, qg_sem)

    def load_w(kz):
        zz = flip(z, kz)
        return pltpu.make_async_copy(w_hbm.at[pl.ds(pl.multiple_of(zz * (X * B), X * B), X * B), :], w.at[zz], w_sem.at[kz])

    def own():
        return pltpu.make_async_copy(lat_ref, lat.at[z, x], own_sem)

    bits = [1 << i for i in range(int(math.log2(Z)))][::-1]
    order = [sum(((k >> i) & 1) << (len(bits) - 1 - i) for i in range(len(bits))) for k in range(Z)]
    far = order[1:][::-1][::-1]
    load_qg().start()
    for kz in order:
        load_w(kz).start()
    own().start()

    barrier = pltpu.get_barrier_semaphore()
    peers = [(y * CORES + 1 - core, head)]
    peers += [(flip(y, k) * CORES + core, head) for k in range(1, Y)]
    peers += [(dp, flip(z, k) * X + x) for k in range(1, Z)]
    peers += [(dp, z * X + flip(x, k)) for k in range(1, X)]
    for peer in peers:
        pl.semaphore_signal(barrier, inc=1, device_id=peer, device_id_type=MESH)
    pl.semaphore_wait(barrier, len(peers))

    def send_az(kz, bit):
        zz = flip(z, kz)
        return pltpu.make_async_remote_copy(
            src_ref=lat.at[zz, x], dst_ref=lat.at[zz, x],
            send_sem=az_s.at[kz ^ bit], recv_sem=az_r.at[kz ^ bit],
            device_id=(dp, flip(z, bit) * X + x), device_id_type=MESH)

    def recv_az(kz):
        zz = flip(z, kz)
        return pltpu.make_async_remote_copy(
            src_ref=lat.at[zz, x], dst_ref=lat.at[zz, x],
            send_sem=az_s.at[kz], recv_sem=az_r.at[kz],
            device_id=(dp, flip(z, kz & -kz) * X + x), device_id_type=MESH)

    def send_ax(kz, kx):
        zz = flip(z, kz)
        return pltpu.make_async_remote_copy(
            src_ref=lat.at[zz, x], dst_ref=lat.at[zz, x],
            send_sem=ax_s.at[kz, kx], recv_sem=ax_r.at[kz, kx],
            device_id=(dp, z * X + flip(x, kx)), device_id_type=MESH)

    def recv_ax(kz, kx):
        zz = flip(z, kz)
        xx = flip(x, kx)
        return pltpu.make_async_remote_copy(
            src_ref=lat.at[zz, xx], dst_ref=lat.at[zz, xx],
            send_sem=ax_s.at[kz, kx], recv_sem=ax_r.at[kz, kx],
            device_id=(dp, z * X + xx), device_id_type=MESH)

    def low(kz):
        return [b for b in bits if kz == 0 or b < (kz & -kz)]

    def forward(kz):
        if kz:
            recv_az(kz).wait_recv()
        for bit in low(kz):
            send_az(kz, bit).start()
        for kx in range(1, X):
            send_ax(kz, kx).start()

    def send_lx(kz, kx):
        zz, xx = flip(z, kz), flip(x, kx)
        return pltpu.make_async_remote_copy(
            src_ref=plat.at[zz, xx], dst_ref=xbuf.at[kx - 1, kz],
            send_sem=lx_s.at[kz, kx], recv_sem=lx_r.at[kz, kx],
            device_id=(dp, z * X + xx), device_id_type=MESH)

    def send_lz(kz):
        zz = flip(z, kz)
        return pltpu.make_async_remote_copy(
            src_ref=plat.at[zz, x], dst_ref=zbuf.at[kz - 1],
            send_sem=lz_s.at[kz], recv_sem=lz_r.at[kz],
            device_id=(dp, zz * X + x), device_id_type=MESH)

    def lat_share(kz):
        zz = flip(z, kz)

        @pl.loop(0, NT)
        def _(t):
            cols = pl.ds(pl.multiple_of(t * T, T), T)
            res = lax.dot_general(w[zz], qg[cols, :], (((1,), (1,)), ((), ())), preferred_element_type=f32)
            plat[zz, :, :, cols] = res.astype(jnp.bfloat16).reshape(X, B, T)

        for kx in range(1, X):
            send_lx(kz, kx).start()

    def lat_sum_x(kz):
        zz = flip(z, kz)
        for kx in range(1, X):
            send_lx(kz, kx).wait_recv()
        total = plat[zz, x].astype(f32)
        for kx in range(1, X):
            total = total + xbuf[kx - 1, kz].astype(f32)
        if kz:
            plat[zz, x] = total.astype(jnp.bfloat16)
            send_lz(kz).start()
        else:
            for k in range(1, Z):
                send_lz(k).wait_recv()
                total = total + zbuf[k - 1].astype(f32)
            lg_ref[...] = total.astype(jnp.bfloat16)

    def send_ws(g, c):
        p = lax.div(g, CORES)
        return pltpu.make_async_remote_copy(
            src_ref=part.at[g, c], dst_ref=sib.at[p, c],
            send_sem=ws_s.at[p, c], recv_sem=ws_r.at[p, c],
            device_id=(y * CORES + 1 - core, head), device_id_type=MESH)

    def send_wy(p, c):
        slot = lax.rem(y - p + Y, Y) - 1
        return pltpu.make_async_remote_copy(
            src_ref=part.at[p * CORES + core, c], dst_ref=ybuf.at[slot, c],
            send_sem=wy_s.at[slot, c], recv_sem=wy_r.at[slot, c],
            device_id=(p * CORES + core, head), device_id_type=MESH)

    def w_share(kz):
        zz = flip(z, kz)
        for kx in range(1, X):
            recv_ax(kz, kx).wait_recv()
        for r in range(R):
            g = zz * R + r

            @pl.loop(0, NC)
            def _(c):
                cols = pl.ds(pl.multiple_of(c * C, C), C)
                left = lat[zz].reshape(X * B, -1)[r * rows:(r + 1) * rows, :]
                res = jnp.dot(left, qg[:, cols], preferred_element_type=f32)
                part[g, c] = res.astype(jnp.bfloat16)

                @pl.when(lax.rem(g, CORES) != core)
                def _():
                    send_ws(g, c).start()

    def w_sum(kz):
        zz = flip(z, kz)
        for r in range(R):
            g = zz * R + r
            p = lax.div(g, CORES)

            @pl.when((lax.rem(g, CORES) == core) & (p != y))
            def _():
                @pl.loop(0, NC)
                def _(c):
                    send_ws(g, c).wait_recv()
                    total = part[g, c].astype(f32) + sib[p, c].astype(f32)
                    part[g, c] = total.astype(jnp.bfloat16)
                    send_wy(p, c).start()

    def q_out(t, c):
        return pltpu.make_async_copy(
            qs.at[t, c],
            q_hbm.at[pl.ds(pl.multiple_of(t * TQ, TQ), TQ), pl.ds(pl.multiple_of(c * C, C), C)],
            q_sem.at[t, c])

    def queries():
        @pl.loop(0, NQ)
        def _(t):
            toks = pl.ds(pl.multiple_of(t * TQ, TQ), TQ)
            lhs[...] = lat[:, :, :, toks].reshape(D, TQ).T

            @pl.loop(0, NC)
            def _(c):
                cols = pl.ds(pl.multiple_of(c * C, C), C)
                res = jnp.dot(lhs[...], w[:, :, cols].reshape(D, C), preferred_element_type=f32)
                qs[t, c] = res.astype(jnp.bfloat16)
                q_out(t, c).start()

    own().wait()
    forward(0)
    load_qg().wait()
    seq = order[1:] + [0]
    for kz in order:
        load_w(kz).wait()
    lat_share(seq[0])
    w_share(0)
    w_sum(0)
    done = {seq[0]}
    arrive = sorted(range(1, Z), key=lambda k: (bin(k).count("1"), k))
    for kz in arrive:
        forward(kz)
        nxt = [k for k in seq if k not in done]
        if nxt:
            lat_share(nxt[0])
            done.add(nxt[0])
    for kz in seq:
        if kz not in done:
            lat_share(kz)
    for kz in order[1:]:
        w_share(kz)
        w_sum(kz)
    for kz in order[1:]:
        lat_sum_x(kz)
    queries()
    lat_sum_x(0)

    @pl.loop(0, NC)
    def _(c):
        mine = y * CORES + core
        send_ws(mine, c).wait_recv()
        total = part[mine, c].astype(f32) + sib[y, c].astype(f32)
        for k in range(1, Y):
            p = lax.rem(y + k, Y)
            other = pltpu.make_async_remote_copy(
                src_ref=part.at[p * CORES + core, c], dst_ref=ybuf.at[k - 1, c],
                send_sem=wy_s.at[k - 1, c], recv_sem=wy_r.at[k - 1, c],
                device_id=(p * CORES + core, head), device_id_type=MESH)
            other.wait_recv()
            total = total + ybuf[k - 1, c].astype(f32)
        grad_ref[:, pl.ds(pl.multiple_of(c * C, C), C)] = total

    for kz in range(Z):
        for bit in low(kz):
            send_az(kz, bit).wait_send()
        for kx in range(1, X):
            send_ax(kz, kx).wait_send()
            send_lx(kz, kx).wait_send()
        if kz:
            send_lz(kz).wait_send()

    @pl.loop(0, NC)
    def _(c):
        for p in range(Y):
            send_ws(p * CORES + 1 - core, c).wait_send()
        for k in range(1, Y):
            send_wy(lax.rem(y - k + Y, Y), c).wait_send()
        for t in range(NQ):
            q_out(t, c).wait()


def on_device(n_dp, n_head, latent, weight, query_grad, master, first_moment, second_moment):
    T_all, B = latent.shape
    D, width = weight.shape
    X = 1 << (int(math.log2(n_head)) // 2)
    Z = n_head // X
    Y = n_dp // CORES
    R = n_dp // Z
    rows = D // n_dp
    C = 1024 if width % 1024 == 0 else 512
    NC = width // C
    T = min(256, T_all)
    NT = T_all // T
    TQ = min(512, T_all)
    NQ = T_all // TQ
    bf = jnp.bfloat16
    sem = pltpu.SemaphoreType.DMA
    vmem = pl.BlockSpec(memory_space=pltpu.VMEM)
    hbm = pl.BlockSpec(memory_space=pl.ANY)
    queries, lgt, grad = pl.pallas_call(
        functools.partial(kernel, (Z, X, Y, R, NC, C, NT, T, NQ, TQ)),
        out_shape=(
            jax.ShapeDtypeStruct((T_all, width), bf),
            jax.ShapeDtypeStruct((B, T_all), bf),
            jax.ShapeDtypeStruct((rows, width), jnp.float32),
        ),
        in_specs=[vmem, hbm, hbm],
        out_specs=(hbm, vmem, vmem),
        scratch_shapes=[
            pltpu.VMEM((Z, X * B, width), bf),
            pltpu.VMEM((T_all, width), bf),
            pltpu.VMEM((Z, X, B, T_all), bf),
            pltpu.VMEM((n_dp, NC, rows, C), bf),
            pltpu.VMEM((Y, NC, rows, C), bf),
            pltpu.VMEM((max(Y - 1, 1), NC, rows, C), bf),
            pltpu.VMEM((Z, X, B, T_all), bf),
            pltpu.VMEM((X - 1, Z, B, T_all), bf),
            pltpu.VMEM((Z - 1, B, T_all), bf),
            pltpu.VMEM((TQ, D), bf),
            pltpu.VMEM((NQ, NC, TQ, C), bf),
            sem((Z,)), sem, sem, sem((NQ, NC)),
            sem((Z,)), sem((Z,)), sem((Z, X)), sem((Z, X)),
            sem((Z, X)), sem((Z, X)), sem((Z,)), sem((Z,)),
            sem((Y, NC)), sem((Y, NC)), sem((max(Y - 1, 1), NC)), sem((max(Y - 1, 1), NC)),
        ],
        compiler_params=pltpu.CompilerParams(
            collective_id=0, has_side_effects=True, vmem_limit_bytes=60 * 1024 * 1024
        ),
        cost_estimate=pl.CostEstimate(
            flops=6 * T_all * D * width, bytes_accessed=4 * (D + T_all) * width, transcendentals=0
        ),
    )(latent.T, weight, query_grad)
    latent_grad = lgt.T
    new_first = 0.9 * first_moment + 0.1 * grad
    new_second = 0.95 * second_moment + 0.05 * grad * grad
    first_hat = new_first / (1.0 - 0.9**STEP)
    second_hat = new_second / (1.0 - 0.95**STEP)
    new_master = master - 0.01 * (first_hat / (jnp.sqrt(second_hat) + 1e-08) + 0.1 * master)
    return (queries, latent_grad, new_master, new_first, new_second)


def solution(mesh):
    return jax.shard_map(
        functools.partial(on_device, mesh.shape["dp"], mesh.shape["head"]),
        mesh=mesh,
        in_specs=(P("dp", "head"), P(None, "head")) + (P("dp", "head"),) * 4,
        out_specs=(P("dp", "head"),) * 5,
        check_vma=False,
    )
```

```python
import functools
import math

import jax
import jax.numpy as jnp
from jax import lax
from jax.experimental import pallas as pl
from jax.experimental.pallas import tpu as pltpu
from jax.sharding import PartitionSpec as P

STEP = 10
CORES = 2
MESH = pl.DeviceIdType.MESH


def flip(a, k):
    out = a
    b = 1
    while b <= k:
        if k & b:
            out = out + b * (1 - 2 * lax.rem(lax.div(a, b), 2))
        b *= 2
    return out


def kernel(sizes, lat_ref, w_hbm, qg_hbm, q_hbm, lg_ref, grad_ref,
           w, qg, lat, part, sib, ybuf, plat, xbuf, zbuf, lhs, qs,
           w_sem, qg_sem, own_sem, q_sem,
           az_s, az_r, ax_s, ax_r, lx_s, lx_r, lz_s, lz_r, ws_s, ws_r, wy_s, wy_r):
    Z, X, Y, Q, NC, C, NT, T, NQ, TQ = sizes
    dp = lax.axis_index("dp")
    head = lax.axis_index("head")
    y, core = lax.div(dp, CORES), lax.rem(dp, CORES)
    z, x = lax.div(head, X), lax.rem(head, X)
    D = w_hbm.shape[0]
    B = lat.shape[2]
    f32 = jnp.float32

    def load_qg():
        return pltpu.make_async_copy(qg_hbm, qg, qg_sem)

    def load_w(kz):
        zz = flip(z, kz)
        return pltpu.make_async_copy(w_hbm.at[pl.ds(pl.multiple_of(zz * (X * B), X * B), X * B), :], w.at[zz], w_sem.at[kz])

    def own():
        return pltpu.make_async_copy(lat_ref, lat.at[z, x], own_sem)

    bits = [1 << i for i in range(int(math.log2(Z)))][::-1]
    order = [sum(((k >> i) & 1) << (len(bits) - 1 - i) for i in range(len(bits))) for k in range(Z)]
    load_qg().start()
    for kz in order:
        load_w(kz).start()
    own().start()

    barrier = pltpu.get_barrier_semaphore()
    peers = [(y * CORES + 1 - core, head)]
    peers += [(flip(y, k) * CORES + core, head) for k in range(1, Y)]
    peers += [(dp, flip(z, k) * X + x) for k in range(1, Z)]
    peers += [(dp, z * X + flip(x, k)) for k in range(1, X)]
    for peer in peers:
        pl.semaphore_signal(barrier, inc=1, device_id=peer, device_id_type=MESH)
    pl.semaphore_wait(barrier, len(peers))

    def send_az(kz, bit):
        zz = flip(z, kz)
        return pltpu.make_async_remote_copy(
            src_ref=lat.at[zz, x], dst_ref=lat.at[zz, x],
            send_sem=az_s.at[kz ^ bit], recv_sem=az_r.at[kz ^ bit],
            device_id=(dp, flip(z, bit) * X + x), device_id_type=MESH)

    def recv_az(kz):
        zz = flip(z, kz)
        return pltpu.make_async_remote_copy(
            src_ref=lat.at[zz, x], dst_ref=lat.at[zz, x],
            send_sem=az_s.at[kz], recv_sem=az_r.at[kz],
            device_id=(dp, flip(z, kz & -kz) * X + x), device_id_type=MESH)

    def send_ax(kz, kx):
        zz = flip(z, kz)
        return pltpu.make_async_remote_copy(
            src_ref=lat.at[zz, x], dst_ref=lat.at[zz, x],
            send_sem=ax_s.at[kz, kx], recv_sem=ax_r.at[kz, kx],
            device_id=(dp, z * X + flip(x, kx)), device_id_type=MESH)

    def recv_ax(kz, kx):
        zz = flip(z, kz)
        xx = flip(x, kx)
        return pltpu.make_async_remote_copy(
            src_ref=lat.at[zz, xx], dst_ref=lat.at[zz, xx],
            send_sem=ax_s.at[kz, kx], recv_sem=ax_r.at[kz, kx],
            device_id=(dp, z * X + xx), device_id_type=MESH)

    def low(kz):
        return [b for b in bits if kz == 0 or b < (kz & -kz)]

    def forward(kz):
        if kz:
            recv_az(kz).wait_recv()
        for bit in low(kz):
            send_az(kz, bit).start()
        for kx in range(1, X):
            send_ax(kz, kx).start()

    def send_lx(kz, kx):
        zz, xx = flip(z, kz), flip(x, kx)
        return pltpu.make_async_remote_copy(
            src_ref=plat.at[zz, xx], dst_ref=xbuf.at[kx - 1, kz],
            send_sem=lx_s.at[kz, kx], recv_sem=lx_r.at[kz, kx],
            device_id=(dp, z * X + xx), device_id_type=MESH)

    def send_lz(kz):
        zz = flip(z, kz)
        return pltpu.make_async_remote_copy(
            src_ref=plat.at[zz, x], dst_ref=zbuf.at[kz - 1],
            send_sem=lz_s.at[kz], recv_sem=lz_r.at[kz],
            device_id=(dp, zz * X + x), device_id_type=MESH)

    def lat_share(kz):
        zz = flip(z, kz)

        @pl.loop(0, NT)
        def _(t):
            cols = pl.ds(pl.multiple_of(t * T, T), T)
            res = lax.dot_general(w[zz], qg[cols, :], (((1,), (1,)), ((), ())), preferred_element_type=f32)
            plat[zz, :, :, cols] = res.astype(jnp.bfloat16).reshape(X, B, T)

        for kx in range(1, X):
            send_lx(kz, kx).start()

    def lat_sum_x(kz):
        zz = flip(z, kz)
        for kx in range(1, X):
            send_lx(kz, kx).wait_recv()
        total = plat[zz, x].astype(f32)
        for kx in range(1, X):
            total = total + xbuf[kx - 1, kz].astype(f32)
        if kz:
            plat[zz, x] = total.astype(jnp.bfloat16)
            send_lz(kz).start()
        else:
            for k in range(1, Z):
                send_lz(k).wait_recv()
                total = total + zbuf[k - 1].astype(f32)
            lg_ref[...] = total.astype(jnp.bfloat16)

    def send_ws(h, c):
        p, j = lax.div(h, Q * CORES), lax.rem(h, Q)
        return pltpu.make_async_remote_copy(
            src_ref=part.at[h, c], dst_ref=sib.at[p, j, c],
            send_sem=ws_s.at[p, j, c], recv_sem=ws_r.at[p, j, c],
            device_id=(y * CORES + 1 - core, head), device_id_type=MESH)

    def copy_wy(h, p, slot, c):
        j = lax.rem(h, Q)
        return pltpu.make_async_remote_copy(
            src_ref=part.at[h, c], dst_ref=ybuf.at[slot, j, c],
            send_sem=wy_s.at[slot, j, c], recv_sem=wy_r.at[slot, j, c],
            device_id=(p * CORES + core, head), device_id_type=MESH)

    def w_share(kz, kx):
        zz, xx = flip(z, kz), flip(x, kx)
        if kx:
            recv_ax(kz, kx).wait_recv()
        h = zz * X + xx
        g = lax.div(h, Q)

        @pl.loop(0, NC)
        def _(c):
            cols = pl.ds(pl.multiple_of(c * C, C), C)
            res = jnp.dot(lat[zz, xx], qg[:, cols], preferred_element_type=f32)
            part[h, c] = res.astype(jnp.bfloat16)

            @pl.when(lax.rem(g, CORES) != core)
            def _():
                send_ws(h, c).start()

    def w_sum(kz, kx):
        h = flip(z, kz) * X + flip(x, kx)
        g = lax.div(h, Q)
        p = lax.div(g, CORES)

        @pl.when((lax.rem(g, CORES) == core) & (p != y))
        def _():
            @pl.loop(0, NC)
            def _(c):
                send_ws(h, c).wait_recv()
                total = part[h, c].astype(f32) + sib[p, lax.rem(h, Q), c].astype(f32)
                part[h, c] = total.astype(jnp.bfloat16)
                copy_wy(h, p, lax.rem(y - p + Y, Y) - 1, c).start()

    def q_out(t, c):
        return pltpu.make_async_copy(
            qs.at[t, c],
            q_hbm.at[pl.ds(pl.multiple_of(t * TQ, TQ), TQ), pl.ds(pl.multiple_of(c * C, C), C)],
            q_sem.at[t, c])

    def queries():
        @pl.loop(0, NQ)
        def _(t):
            toks = pl.ds(pl.multiple_of(t * TQ, TQ), TQ)
            lhs[...] = lat[:, :, :, toks].reshape(D, TQ).T

            @pl.loop(0, NC)
            def _(c):
                cols = pl.ds(pl.multiple_of(c * C, C), C)
                res = jnp.dot(lhs[...], w[:, :, cols].reshape(D, C), preferred_element_type=f32)
                qs[t, c] = res.astype(jnp.bfloat16)
                q_out(t, c).start()

    own().wait()
    forward(0)
    load_qg().wait()
    xs = list(range(1, X))
    tail = order[1:]
    turns = iter(tail + [0])

    def lat_next():
        kz = next(turns, None)
        if kz is not None:
            lat_share(kz)

    w_share(0, 0)
    for kz in range(Z):
        load_w(kz).wait()
    lat_next()
    w_sum(0, 0)
    for kx in xs:
        w_share(0, kx)
    lat_next()
    for kx in xs:
        w_sum(0, kx)
    once = [k for k in tail if k & (k - 1) == 0]
    twice = [k for k in tail if k & (k - 1)]
    for group in (once, twice):
        for kz in group:
            forward(kz)
        for kz in group:
            w_share(kz, 0)
        for kz in group:
            w_sum(kz, 0)
    lat_next()
    lat_sum_x(tail[0])
    for kz in once:
        for kx in xs:
            w_share(kz, kx)
            w_sum(kz, kx)
    lat_next()
    for kz in twice:
        for kx in xs:
            w_share(kz, kx)
            w_sum(kz, kx)
    for kz in tail[1:]:
        lat_sum_x(kz)
    queries()
    lat_sum_x(0)

    for j in range(Q):
        @pl.loop(0, NC)
        def _(c):
            mine = (y * CORES + core) * Q + j
            send_ws(mine, c).wait_recv()
            total = part[mine, c].astype(f32) + sib[y, j, c].astype(f32)
            for k in range(1, Y):
                copy_wy(mine, lax.rem(y + k, Y), k - 1, c).wait_recv()
                total = total + ybuf[k - 1, j, c].astype(f32)
            grad_ref[j * B:(j + 1) * B, pl.ds(pl.multiple_of(c * C, C), C)] = total

    for kz in range(Z):
        for bit in low(kz):
            send_az(kz, bit).wait_send()
        for kx in range(1, X):
            send_ax(kz, kx).wait_send()
            send_lx(kz, kx).wait_send()
        if kz:
            send_lz(kz).wait_send()

    @pl.loop(0, NC)
    def _(c):
        for j in range(Q):
            for p in range(Y):
                send_ws((p * CORES + 1 - core) * Q + j, c).wait_send()
            for k in range(1, Y):
                p = lax.rem(y - k + Y, Y)
                copy_wy((p * CORES + core) * Q + j, p, k - 1, c).wait_send()
        for t in range(NQ):
            q_out(t, c).wait()


def on_device(n_dp, n_head, latent, weight, query_grad, master, first_moment, second_moment):
    T_all, B = latent.shape
    D, width = weight.shape
    X = 1 << (int(math.log2(n_head)) // 2)
    Z = n_head // X
    Y = n_dp // CORES
    Q = n_head // n_dp
    rows = D // n_dp
    C = 1024 if width % 1024 == 0 else 512
    NC = width // C
    T = min(256, T_all)
    NT = T_all // T
    TQ = min(512, T_all)
    NQ = T_all // TQ
    bf = jnp.bfloat16
    sem = pltpu.SemaphoreType.DMA
    vmem = pl.BlockSpec(memory_space=pltpu.VMEM)
    hbm = pl.BlockSpec(memory_space=pl.ANY)
    queries, lgt, grad = pl.pallas_call(
        functools.partial(kernel, (Z, X, Y, Q, NC, C, NT, T, NQ, TQ)),
        out_shape=(
            jax.ShapeDtypeStruct((T_all, width), bf),
            jax.ShapeDtypeStruct((B, T_all), bf),
            jax.ShapeDtypeStruct((rows, width), jnp.float32),
        ),
        in_specs=[vmem, hbm, hbm],
        out_specs=(hbm, vmem, vmem),
        scratch_shapes=[
            pltpu.VMEM((Z, X * B, width), bf),
            pltpu.VMEM((T_all, width), bf),
            pltpu.VMEM((Z, X, B, T_all), bf),
            pltpu.VMEM((n_head, NC, B, C), bf),
            pltpu.VMEM((Y, Q, NC, B, C), bf),
            pltpu.VMEM((max(Y - 1, 1), Q, NC, B, C), bf),
            pltpu.VMEM((Z, X, B, T_all), bf),
            pltpu.VMEM((X - 1, Z, B, T_all), bf),
            pltpu.VMEM((Z - 1, B, T_all), bf),
            pltpu.VMEM((TQ, D), bf),
            pltpu.VMEM((NQ, NC, TQ, C), bf),
            sem((Z,)), sem, sem, sem((NQ, NC)),
            sem((Z,)), sem((Z,)), sem((Z, X)), sem((Z, X)),
            sem((Z, X)), sem((Z, X)), sem((Z,)), sem((Z,)),
            sem((Y, Q, NC)), sem((Y, Q, NC)), sem((max(Y - 1, 1), Q, NC)), sem((max(Y - 1, 1), Q, NC)),
        ],
        compiler_params=pltpu.CompilerParams(
            collective_id=0, has_side_effects=True, vmem_limit_bytes=60 * 1024 * 1024
        ),
        cost_estimate=pl.CostEstimate(
            flops=6 * T_all * D * width, bytes_accessed=4 * (D + T_all) * width, transcendentals=0
        ),
    )(latent.T, weight, query_grad)
    latent_grad = lgt.T
    new_first = 0.9 * first_moment + 0.1 * grad
    new_second = 0.95 * second_moment + 0.05 * grad * grad
    first_hat = new_first / (1.0 - 0.9**STEP)
    second_hat = new_second / (1.0 - 0.95**STEP)
    new_master = master - 0.01 * (first_hat / (jnp.sqrt(second_hat) + 1e-08) + 0.1 * master)
    return (queries, latent_grad, new_master, new_first, new_second)


def solution(mesh):
    return jax.shard_map(
        functools.partial(on_device, mesh.shape["dp"], mesh.shape["head"]),
        mesh=mesh,
        in_specs=(P("dp", "head"), P(None, "head")) + (P("dp", "head"),) * 4,
        out_specs=(P("dp", "head"),) * 5,
        check_vma=False,
    )
```
